128 devices in a mesh: seq: 4 (over x), exp: 32 (over y, z, core).
Axes of the slice: x: 4, y: 4, z: 4, core: 2. Of those that a mesh axis runs over, the one named last changes fastest.
Arguments:
- tokens: bfloat16 [32, 2048, 768], P('exp', 'seq'), may hold values from -64 to 64
- halt_steps: int32 [32, 2048], P('exp', 'seq'), may hold values from 0 to 4, as said below
- phi: bfloat16 [768, 1024], P(None, 'exp')
- w_up: bfloat16 [128, 768, 3072], P(('seq', 'exp')), may hold values from -0.21875 to 0.21875
- w_down: bfloat16 [128, 3072, 768], P(('seq', 'exp')), may hold values from -0.875 to 0.875
- cotangent: bfloat16 [32, 2048, 768], P('exp', 'seq'), may hold values from -6 to 6
Outputs:
- mixed: bfloat16 [32, 2048, 768], P('exp', 'seq')
- grad_tokens: bfloat16 [32, 2048, 768], P('exp', 'seq')
- grad_phi_t: float32 [1024, 768], P(('seq', 'exp'))
- grad_up: bfloat16 [128, 768, 3072], P(('seq', 'exp'))
- grad_down: bfloat16 [128, 3072, 768], P(('seq', 'exp'))
The draws below stay inside these ranges and needn't reach their ends.
Inputs may be any that keep to these rules, and one draw needn't show every extreme that they name: `halt_steps`: every clip has a token with 4 steps.
All inputs are finite; a program needn't handle non-finite values.
Results may differ from the reference program's by a relative error of at most 0.017.
Values may be sent and summed in bfloat16 or wider, within the bound.
No kernel may reach another device: no remote copies, remote signals or barrier semaphores. Data moves between devices by JAX's collectives and lax.ppermute only.
A program may use at most 128 MiB of HBM per device.

```python
import jax
import jax.numpy as jnp
from jax import lax

D = 768
HID = 3072
PER_EXP = 8
ACT_MAX = 4
LAYER_POS = 1
EXPERTS = 128
SLOTS = 1024
CLIPS = 32
LEN = 2048


def chosen_spots(key):
    key = jax.random.fold_in(key, 202)
    band = LEN // 6
    offsets = jax.random.randint(key, (CLIPS, 6), 0, band)
    return (offsets + jnp.arange(6, dtype=jnp.int32)[None, :] * band).astype(jnp.int32)


def base_phi(key):
    key = jax.random.fold_in(key, 303)
    values = jnp.clip(jax.random.normal(key, (D, SLOTS), jnp.float32), -6.0, 6.0)
    return values * D ** (-0.5)


def draw_phi(key, part):
    values = base_phi(key)
    return values.astype(jnp.bfloat16)


def draw_tokens(key, part):
    own_key = jax.random.fold_in(key, 12)
    first_key = jax.random.fold_in(own_key, 0)
    values = jnp.clip(jax.random.normal(first_key, (CLIPS, LEN, D), jnp.float32), -6.0, 6.0)
    return jnp.clip(values, -64.0, 64.0).astype(jnp.bfloat16)


def draw_halt_steps(key, part):
    spots = chosen_spots(key)
    own_key = jax.random.fold_in(key, 13)
    key_one, key_two, key_three, key_four = jax.random.split(own_key, 4)
    cutoff = jax.random.randint(key_one, (CLIPS, 1), 12, 61)
    uniform_draw = jax.random.randint(key_two, (CLIPS, LEN), 0, 64)
    running = jax.random.randint(key_three, (CLIPS, LEN), LAYER_POS + 1, ACT_MAX + 1)
    halted = jax.random.randint(key_four, (CLIPS, LEN), 0, LAYER_POS + 1)
    steps = jnp.where(uniform_draw < cutoff, running, halted)
    steps = steps.at[jnp.arange(CLIPS)[:, None], spots].set(ACT_MAX)
    return steps.astype(jnp.int32)


def block_scale(stream_key, dims, cuts, smallest, top_value):
    gain, own = 1.0, jax.random.fold_in(stream_key, 6)
    for position, shards_of in cuts:
        steps = jnp.exp(jax.random.uniform(jax.random.fold_in(own, position), (shards_of,), jnp.float32, smallest / len(cuts), top_value / len(cuts)))
        gain = gain * jnp.repeat(steps, dims[position] // shards_of).reshape([-1 if axis == position else 1 for axis in range(len(dims))])
    return gain


def normal_values(stream_key, dims, width, bound, cuts=(), kind=jnp.bfloat16):
    values = jax.random.normal(stream_key, dims, jnp.float32) * width
    if len(cuts) > 0:
        values = block_scale(stream_key, dims, cuts, -0.22, 0.18) * values
    return jnp.clip(values, min=-bound, max=bound).astype(kind)


def setup_inputs(seed: int = 0) -> dict:
    key_of = jax.random.split(jax.random.key(seed), 7)
    return {
        "tokens": draw_tokens(jax.random.fold_in(key_of[6], 71), 0),
        "halt_steps": draw_halt_steps(jax.random.fold_in(key_of[6], 71), 0),
        "phi": draw_phi(jax.random.fold_in(key_of[6], 71), 0),
        "w_up": normal_values(key_of[3], (EXPERTS, D, HID), D ** -0.5, 0.21875, ((0, 128),)),
        "w_down": normal_values(key_of[4], (EXPERTS, HID, D), (HID // 64) ** -0.5, 0.875, ((0, 128),)),
        "cotangent": normal_values(key_of[5], (CLIPS, LEN, D), 1.0, 6.0, ((0, 32), (1, 4))),
    }


EPS = 1e-06
LOW_LOGIT = -1e+30

def rms_factor(values):
    return lax.rsqrt(lax.optimization_barrier(jnp.mean(values * values, axis=-1, keepdims=True)) + EPS)

def by_expert(values):
    return values.reshape(CLIPS, EXPERTS, PER_EXP, D).transpose(1, 0, 2, 3).reshape(EXPERTS, CLIPS * PER_EXP, D)

def by_clip(values):
    return values.reshape(EXPERTS, CLIPS, PER_EXP, D).transpose(1, 0, 2, 3).reshape(CLIPS, SLOTS, D)

def reference(tokens, halt_steps, phi, w_up, w_down, cotangent):
    active = halt_steps > LAYER_POS

    def dispatch(inputs):
        clip_tokens, is_live = inputs
        live_rows = is_live[:, None]
        logits = jnp.dot(clip_tokens, phi, preferred_element_type=jnp.float32)
        slot_top = lax.optimization_barrier(jnp.max(jnp.where(live_rows, logits, LOW_LOGIT), axis=0))
        weights = jnp.where(live_rows, jnp.exp(logits - slot_top), 0.0).astype(jnp.bfloat16)
        slot_total = lax.optimization_barrier(jnp.sum(weights.astype(jnp.float32), axis=0))
        mixed_in = jnp.dot(weights.T, clip_tokens, preferred_element_type=jnp.float32) / slot_total[:, None]
        slot_in = (mixed_in * rms_factor(mixed_in)).astype(jnp.bfloat16)
        return (logits, weights, slot_total, mixed_in, slot_in)
    logits, weights, totals, mixed_in, slot_in = lax.map(dispatch, (tokens, active))

    def expert_forward(inputs):
        expert_rows, up_matrix, down_matrix = inputs
        preact = jnp.dot(expert_rows, up_matrix, preferred_element_type=jnp.float32)
        hidden = jax.nn.gelu(preact).astype(jnp.bfloat16)
        return jnp.dot(hidden, down_matrix, preferred_element_type=jnp.float32).astype(jnp.bfloat16)
    slot_out = by_clip(lax.map(expert_forward, (by_expert(slot_in), w_up, w_down)))

    def combine_step(inputs):
        clip_logits, clip_out, is_live, clip_cot = inputs
        live_rows = is_live[:, None]
        combine = jax.nn.softmax(clip_logits, axis=-1)
        combine_b = combine.astype(jnp.bfloat16)
        mixed = jnp.where(live_rows, jnp.dot(combine_b, clip_out, preferred_element_type=jnp.float32), 0.0).astype(jnp.bfloat16)
        masked_grad = jnp.where(live_rows, clip_cot, jnp.zeros((), jnp.bfloat16))
        combine_grad = jnp.dot(masked_grad, clip_out.T, preferred_element_type=jnp.float32)
        logit_part = combine * (combine_grad - lax.optimization_barrier(jnp.sum(combine * combine_grad, axis=-1, keepdims=True)))
        slot_grad = jnp.dot(combine_b.T, masked_grad, preferred_element_type=jnp.float32).astype(jnp.bfloat16)
        return (mixed, logit_part, slot_grad)
    mixed, logit_part, slot_grad = lax.map(combine_step, (logits, slot_out, active, cotangent))

    def expert_backward(inputs):
        expert_rows, expert_grad, up_matrix, down_matrix = inputs
        preact = jnp.dot(expert_rows, up_matrix, preferred_element_type=jnp.float32)
        hidden = jax.nn.gelu(preact).astype(jnp.bfloat16)
        hidden_grad = jnp.dot(expert_grad, down_matrix.T, preferred_element_type=jnp.float32)
        grad_down = jnp.dot(hidden.T, expert_grad, preferred_element_type=jnp.float32).astype(jnp.bfloat16)
        pre_grad = jax.vjp(jax.nn.gelu, preact)[1](hidden_grad)[0].astype(jnp.bfloat16)
        grad_up = jnp.dot(expert_rows.T, pre_grad, preferred_element_type=jnp.float32).astype(jnp.bfloat16)
        normed_grad = jnp.dot(pre_grad, up_matrix.T, preferred_element_type=jnp.float32).astype(jnp.bfloat16)
        return (grad_up, grad_down, normed_grad)
    grad_up, grad_down, normed_grad = lax.map(expert_backward, (by_expert(slot_in), by_expert(slot_grad), w_up, w_down))
    normed_grad = by_clip(normed_grad)

    def token_backward(carry, inputs):
        clip_tokens, clip_weights, clip_total, clip_mixed, clip_grad_in, clip_logit_part = inputs
        factor = rms_factor(clip_mixed)
        normed = clip_mixed * factor
        returned = clip_grad_in.astype(jnp.float32)
        mixed_grad = (factor * (returned - normed * lax.optimization_barrier(jnp.mean(returned * normed, axis=-1, keepdims=True)))).astype(jnp.bfloat16)
        dispatch_grad = jnp.dot(clip_tokens, mixed_grad.T, preferred_element_type=jnp.float32)
        dispatch_share = clip_weights.astype(jnp.float32) / clip_total
        column_sum = lax.optimization_barrier(jnp.sum(dispatch_share * dispatch_grad, axis=0))
        logit_grad = (clip_logit_part + dispatch_share * (dispatch_grad - column_sum)).astype(jnp.bfloat16)
        share_b = dispatch_share.astype(jnp.bfloat16)
        grad_rows = (jnp.dot(logit_grad, phi.T, preferred_element_type=jnp.float32) + jnp.dot(share_b, mixed_grad, preferred_element_type=jnp.float32)).astype(jnp.bfloat16)
        return (carry + jnp.dot(logit_grad.T, clip_tokens, preferred_element_type=jnp.float32), grad_rows)
    grad_phi_t, grad_tokens = lax.scan(token_backward, jnp.zeros((SLOTS, D), jnp.float32), (tokens, weights, totals, mixed_in, normed_grad, logit_part))
    return (mixed, grad_tokens, grad_phi_t, grad_up, grad_down)
```

```python
import jax
import jax.numpy as jnp
from jax import lax
from jax.sharding import Mesh, PartitionSpec as P

LAYER_POS = 1
EPS = 1e-06
LOW_LOGIT = -1e30

PLANE = ("y", "z")
GROUP = ("y", "z", "core")
CHIPS = ("x", "y", "z")
F32 = jnp.float32
BF16 = jnp.bfloat16


def matmul(a, b, contract):
    return lax.dot_general(a, b, ((contract[:1], contract[1:]), ((), ())), preferred_element_type=F32)


def swap_cores(values):
    return lax.ppermute(values, "core", [(0, 1), (1, 0)])


def along_x(values, steps):
    n = lax.axis_size("x")
    return lax.ppermute(values, "x", [(i, (i + steps) % n) for i in range(n)])


def gather_x(values):
    return [values] + [along_x(values, -k) for k in range(1, lax.axis_size("x"))]


def scatter_x(blocks):
    return [blocks[0]] + [along_x(blocks[k], k) for k in range(1, lax.axis_size("x"))]


def exchange(values, axes):
    return lax.all_to_all(values, axes, 0, 0, tiled=True)


def roll_blocks(blocks, first):
    return lax.dynamic_slice_in_dim(jnp.concatenate([blocks, blocks[:-1]]), first, blocks.shape[0], 0)


def after(values, *others):
    return lax.optimization_barrier((values,) + others)[0]


def gather_phi(phi):
    rows = phi.T
    planes = lax.axis_size("x")
    chips = lax.axis_size("y") * lax.axis_size("z")
    mine = exchange(jnp.broadcast_to(rows[None], (chips,) + rows.shape), PLANE)
    other = swap_cores(mine)
    first = lax.axis_index("core") == 0
    both = jnp.stack([jnp.where(first, mine, other), jnp.where(first, other, mine)], axis=1)
    groups = both.reshape(planes, -1, rows.shape[1])
    return roll_blocks(groups, lax.axis_index("x"))


def per_device(tokens, halt_steps, phi, w_up, w_down, cotangent):
    clip_part = tokens[0]
    features = clip_part.shape[1]
    live_rows = (halt_steps[0] > LAYER_POS)[:, None]
    planes = lax.axis_size("x")
    experts = lax.axis_size("y") * lax.axis_size("z") * lax.axis_size("core")
    here = lax.axis_index("x")

    phi_groups = gather_phi(phi)
    own_slots = phi_groups.shape[1]
    per_expert = own_slots // experts
    phi_all = phi_groups.reshape(-1, features)
    logits = matmul(clip_part, phi_all, (1, 1))

    def group(values, k):
        return values[..., k * own_slots : (k + 1) * own_slots]

    local_top = jnp.max(jnp.where(live_rows, logits, LOW_LOGIT), axis=0)
    weights = jnp.where(live_rows, jnp.exp(logits - local_top), 0.0).astype(BF16)
    local_total = jnp.sum(weights.astype(F32), axis=0)
    part_sums = matmul(weights, clip_part, (0, 0)).astype(BF16).reshape(planes, own_slots, features)
    arrived_sums = scatter_x(part_sums)
    stats = jnp.stack([local_top, local_total])
    all_stats = jnp.stack([jnp.roll(s, k * own_slots, axis=1) for k, s in enumerate(gather_x(stats))])
    slot_top = jnp.max(all_stats[:, 0], axis=0)
    scales = jnp.exp(all_stats[:, 0] - slot_top)
    slot_total = jnp.sum(all_stats[:, 1] * scales, axis=0)
    share_scale = scales[0] / slot_total
    own_scales = group(scales / slot_total, 0)
    mixed_in = sum(
        arrived_sums[k].astype(F32) * own_scales[(planes - k) % planes][:, None] for k in range(planes)
    )
    factor = lax.rsqrt(jnp.mean(mixed_in * mixed_in, axis=-1, keepdims=True) + EPS)
    normed = mixed_in * factor
    slot_in = normed.astype(BF16)
    expert_in = exchange(slot_in.reshape(experts, per_expert, features), GROUP).reshape(-1, features)

    combine = jax.nn.softmax(logits, axis=-1)
    combine_b = combine.astype(BF16)
    masked_grad = jnp.where(live_rows, cotangent[0], jnp.zeros((), BF16))
    part_grads = matmul(combine_b, masked_grad, (0, 0)).astype(BF16).reshape(planes, own_slots, features)
    part_grads = after(part_grads, *arrived_sums)
    slot_grad = sum(g.astype(F32) for g in scatter_x(part_grads)).astype(BF16)
    expert_grad = exchange(slot_grad.reshape(experts, per_expert, features), GROUP).reshape(-1, features)

    up_matrix, down_matrix = w_up[0], w_down[0]
    preact = matmul(expert_in, up_matrix, (1, 0))
    hidden = jax.nn.gelu(preact).astype(BF16)
    output = matmul(hidden, down_matrix, (1, 0)).astype(BF16)
    own_out = exchange(output.reshape(experts, per_expert, features), GROUP).reshape(own_slots, features)

    hidden_grad = matmul(expert_grad, down_matrix, (1, 1))
    pre_grad = jax.vjp(jax.nn.gelu, preact)[1](hidden_grad)[0].astype(BF16)
    normed_grad = matmul(pre_grad, up_matrix, (1, 1)).astype(BF16)
    back_grad = exchange(normed_grad.reshape(experts, per_expert, features), GROUP)
    grad_down = matmul(hidden, expert_grad, (0, 0)).astype(BF16)
    grad_up = matmul(expert_in, pre_grad, (0, 0)).astype(BF16)

    slot_outs = gather_x(own_out)
    mixed = sum(matmul(group(combine_b, k), slot_outs[k], (1, 0)) for k in range(planes))
    mixed = jnp.where(live_rows, mixed, 0.0).astype(BF16)
    combine_grads = [matmul(masked_grad, block, (1, 1)) for block in slot_outs]
    row_sum = sum(
        jnp.sum(group(combine, k) * combine_grads[k], axis=-1, keepdims=True) for k in range(planes)
    )

    back_grad = back_grad.reshape(own_slots, features).astype(F32)
    mixed_grad = (
        factor * (back_grad - normed * jnp.mean(back_grad * normed, axis=-1, keepdims=True))
    ).astype(BF16)
    own_column = jnp.sum(mixed_in * mixed_grad.astype(F32), axis=-1)
    all_grads = gather_x(mixed_grad)
    column_sums = gather_x(own_column)
    part_phi, shares, logit_grads = [], [], []
    for k in range(planes):
        dispatch_grad = matmul(clip_part, all_grads[k], (1, 1))
        dispatch_share = group(weights, k).astype(F32) * group(share_scale, k)
        logit_grad = (
            group(combine, k) * (combine_grads[k] - row_sum)
            + dispatch_share * (dispatch_grad - column_sums[k])
        ).astype(BF16)
        part_phi.append(matmul(logit_grad, clip_part, (0, 0)).astype(BF16))
        shares.append(dispatch_share.astype(BF16))
        logit_grads.append(logit_grad)

    halves = jnp.stack(part_phi).reshape(planes, -1, 2, per_expert, features)
    halves = roll_blocks(halves, lax.rem(planes - here, planes)).reshape((-1,) + halves.shape[2:])
    first = lax.axis_index("core") == 0
    keep = jnp.where(first, halves[:, 0], halves[:, 1])
    give = jnp.where(first, halves[:, 1], halves[:, 0])
    chip_sum = (keep.astype(F32) + swap_cores(give).astype(F32)).astype(BF16)
    grad_phi_t = jnp.sum(exchange(chip_sum, CHIPS).astype(F32), axis=0)

    logit_grads = after(tuple(logit_grads), chip_sum)
    grad_rows = sum(
        matmul(g, p, (1, 0)) + matmul(s, a, (1, 0))
        for g, p, s, a in zip(logit_grads, phi_groups, shares, all_grads)
    )
    return (mixed[None], grad_rows.astype(BF16)[None], grad_phi_t, grad_up[None], grad_down[None])


def solution(mesh):
    fine = Mesh(mesh.devices.reshape(4, 4, 4, 2), ("x", "y", "z", "core"))
    rows = P(GROUP, "x", None)
    blocks = P(("x",) + GROUP, None, None)
    return jax.shard_map(
        per_device,
        mesh=fine,
        in_specs=(rows, P(GROUP, "x"), P(None, GROUP), blocks, blocks, rows),
        out_specs=(rows, rows, P(("x",) + GROUP, None), blocks, blocks),
        check_vma=False,
    )
```

```python
import functools
import math

import jax
import jax.numpy as jnp
from jax import lax
from jax.experimental import pallas as pl
from jax.experimental.pallas import tpu as pltpu
from jax.sharding import Mesh, PartitionSpec as P

LAYER_POS = 1
EPS = 1e-06
LOW_LOGIT = -1e30

PLANE = ("y", "z")
GROUP = ("y", "z", "core")
F32 = jnp.float32
BF16 = jnp.bfloat16


def matmul(a, b, contract):
    return lax.dot_general(a, b, ((contract[:1], contract[1:]), ((), ())), preferred_element_type=F32)


def swap_cores(values):
    return lax.ppermute(values, "core", [(0, 1), (1, 0)])


def along_x(values, steps):
    n = lax.axis_size("x")
    return lax.ppermute(values, "x", [(i, (i + steps) % n) for i in range(n)])


def gather_x(values):
    return [values] + [along_x(values, -k) for k in range(1, lax.axis_size("x"))]


def to_neighbours(values):
    return along_x(values, -1), along_x(values, 1)


def pass_on(ahead, behind):
    half = ahead.shape[0] // 2
    return along_x(behind[:half], 1), along_x(ahead[half:], -1)


def exchange(values, axes):
    return lax.all_to_all(values, axes, 0, 0, tiled=True)


def roll_blocks(blocks, first):
    return lax.dynamic_slice_in_dim(jnp.concatenate([blocks, blocks[:-1]]), first, blocks.shape[0], 0)


def gather_phi(phi):
    rows = phi.T
    planes = lax.axis_size("x")
    chips = lax.axis_size("y") * lax.axis_size("z")
    mine = exchange(jnp.broadcast_to(rows[None], (chips,) + rows.shape), PLANE)
    other = swap_cores(mine)
    first = lax.axis_index("core") == 0
    both = jnp.stack([jnp.where(first, mine, other), jnp.where(first, other, mine)], axis=1)
    groups = both.reshape(planes, -1, rows.shape[1])
    return roll_blocks(groups, lax.axis_index("x"))


def gelu_parts(v):
    scale = math.sqrt(2.0 / math.pi)
    square = v * v
    t = jnp.tanh(scale * v * (1.0 + 0.044715 * square))
    half = 0.5 * (1.0 + t)
    slope = half + 0.5 * scale * v * (1.0 - t * t) * (1.0 + 3.0 * 0.044715 * square)
    return v * half, slope


def unit(*arrays):
    return sum(a[0, 0].astype(BF16) * 0 for a in arrays) + jnp.ones((), BF16)


LIMIT = 56 * 1024 * 1024


def call(kernel, steps, inputs, outputs, scratch=(), work=1000):
    def spec(block, where):
        if where is None:
            where = (0,) * len(block)
        if isinstance(where, tuple):
            return pl.BlockSpec(block, lambda i: where)
        return pl.BlockSpec(block, lambda i: tuple(i if d == where else 0 for d in range(len(block))))

    return pl.pallas_call(
        kernel,
        grid=(steps,),
        in_specs=[spec(block, where) for _, block, where in inputs],
        out_specs=[spec(block, where) for _, _, block, where in outputs],
        out_shape=[jax.ShapeDtypeStruct(shape, kind) for kind, shape, _, _ in outputs],
        scratch_shapes=list(scratch),
        compiler_params=pltpu.CompilerParams(vmem_limit_bytes=LIMIT),
        cost_estimate=pl.CostEstimate(flops=work, bytes_accessed=1000, transcendentals=0),
    )(*[array for array, _, _ in inputs])


def accumulate(total, part, out_ref):
    step = pl.program_id(0)

    @pl.when(step == 0)
    def _():
        total[...] = part

    @pl.when(step > 0)
    def _():
        total[...] += part

    @pl.when(step == pl.num_programs(0) - 1)
    def _():
        out_ref[...] = total[...].astype(BF16)


def forward_kernel(rows_ref, up_ref, down_ref, hidden_ref, slope_ref, out_ref, total):
    preact = jnp.dot(rows_ref[...], up_ref[...], preferred_element_type=F32)
    hidden, slope = gelu_parts(preact)
    hidden = hidden.astype(BF16)
    hidden_ref[...] = hidden
    slope_ref[...] = slope.astype(BF16)
    accumulate(total, jnp.dot(hidden, down_ref[...], preferred_element_type=F32), out_ref)


def backward_kernel(grad_ref, slope_ref, up_ref, down_ref, pre_ref, out_ref, total):
    pre_grad = (slope_ref[...].astype(F32) * matmul(grad_ref[...], down_ref[...], (1, 1))).astype(BF16)
    pre_ref[...] = pre_grad
    accumulate(total, matmul(pre_grad, up_ref[...], (1, 1)), out_ref)


def product_kernel(a_ref, b_ref, out_ref):
    out_ref[...] = matmul(a_ref[...], b_ref[...], (0, 0)).astype(BF16)


def dispatch_kernel(
    phi_ref, tops_ref, norms_ref, *refs
):
    pieces, outs = refs[:5], refs[5:]
    weights_ref, combine_ref, in_ref, normed_ref, factor_ref, inverse_ref, top_ref, logits = outs
    phi = phi_ref[...]
    spans, at = [], 0
    for p in pieces:
        spans.append(slice(at, at + p.shape[0]))
        at += p.shape[0]
    top = None
    for p, span in zip(pieces, spans):
        l = matmul(phi, p[...], (1, 1))
        logits[:, span] = l
        norms = norms_ref[:, span]
        combine_ref[:, span] = (jnp.exp(l - tops_ref[:, span]) * norms).astype(BF16)
        here = jnp.max(jnp.where(norms > 0.0, l, LOW_LOGIT), axis=1, keepdims=True)
        top = here if top is None else jnp.maximum(top, here)
    slot_total, mixed = 0.0, 0.0
    for p, span in zip(pieces, spans):
        w = jnp.where(norms_ref[:, span] > 0.0, jnp.exp(logits[:, span] - top), 0.0).astype(BF16)
        weights_ref[:, span] = w
        slot_total += jnp.sum(w.astype(F32), axis=1, keepdims=True)
        mixed += jnp.dot(w, p[...], preferred_element_type=F32)
    inverse = 1.0 / slot_total
    mixed = mixed * inverse
    factor = lax.rsqrt(jnp.mean(mixed * mixed, axis=1, keepdims=True) + EPS)
    normed = mixed * factor
    normed_ref[...] = normed
    in_ref[...] = normed.astype(BF16)
    factor_ref[...] = factor
    inverse_ref[...] = inverse
    top_ref[...] = top


def slot_kernel(combine_ref, *refs):
    *pieces, out_ref = refs
    total, at = 0.0, 0
    for p in pieces:
        total += jnp.dot(combine_ref[:, at : at + p.shape[0]], p[...], preferred_element_type=F32)
        at += p.shape[0]
    out_ref[...] = total.astype(BF16)


def split(values):
    parts = []
    for _ in range(3):
        part = values.astype(BF16).astype(F32)
        parts.append(part)
        values = values - part
    return parts


def as_row(column):
    return jnp.transpose(jnp.broadcast_to(column, (column.shape[0], 128)))[:1]


def slot_grad_kernel(out_ref, _, combine_ref, top_ref, inverse_ref, *refs):
    *pieces, combine_grad_ref, message_ref, lines = refs
    own, at = out_ref[...], 0
    slots = own.shape[0]
    message_ref[:slots, :] = own
    lines[...] = jnp.zeros_like(lines)
    width = pieces[0].shape[0]
    for p in pieces:
        span = slice(at, at + p.shape[0])
        grad = matmul(own, p[...], (1, 1))
        combine_grad_ref[:, span] = grad
        sums = jnp.sum(combine_ref[:, span].astype(F32) * grad, axis=0, keepdims=True)
        line, start = at // width, at % width
        for k, part in enumerate(split(sums)):
            lines[4 * k + line : 4 * k + line + 1, start : start + p.shape[0]] = part
        at += p.shape[0]
    for line, ref in ((12, top_ref), (13, inverse_ref)):
        for k, part in enumerate(split(as_row(ref[...]))):
            lines[line : line + 1, k * slots : (k + 1) * slots] = part
    message_ref[slots:, :] = lines[...].astype(BF16)


def mixed_grad_kernel(back_ref, normed_ref, factor_ref, _, out_ref, column_ref):
    back = back_ref[...].astype(F32)
    normed, factor = normed_ref[...], factor_ref[...]
    out = (factor * (back - normed * jnp.mean(back * normed, axis=1, keepdims=True))).astype(BF16)
    slots = out.shape[0]
    out_ref[:slots, :] = out
    column = jnp.sum(normed * out.astype(F32), axis=1, keepdims=True) / factor
    column_ref[...] = column
    row = jnp.concatenate(split(as_row(column)), axis=1)
    out_ref[slots:, :] = jnp.broadcast_to(row, (16, row.shape[1])).astype(BF16)


def phi_kernel(grad_ref, combine_ref, combine_grad_ref, weights_ref, inverse_ref, column_ref, *refs):
    messages, pieces, out_ref = refs[:4], refs[4:9], refs[9]
    grad = grad_ref[...]
    width = pieces[0].shape[0]
    messages = [m[...].astype(F32) for m in messages]
    total, at = 0.0, 0
    for p in pieces:
        span = slice(at, at + p.shape[0])
        line, start = at // width, at % width
        at += p.shape[0]
        rows = 0.0
        for k, m in enumerate(messages):
            for j in range(3):
                i = 4 * j + (line - k) % 4
                rows += m[i : i + 1, start : start + p.shape[0]]
        tokens = p[...]
        share = weights_ref[:, span].astype(F32) * inverse_ref[...]
        logit_grad = combine_ref[:, span].astype(F32) * (combine_grad_ref[:, span] - rows) + share * (
            matmul(grad, tokens, (1, 1)) - column_ref[...]
        )
        total += jnp.dot(logit_grad.astype(BF16), tokens, preferred_element_type=F32)
    out_ref[...] = total.astype(BF16)


def combine_kernel(live_ref, tokens_ref, grad_ref, phi_ref, *refs):
    *outs, mixed_ref, logit_ref = refs
    width = outs[0].shape[0]
    logits = matmul(tokens_ref[...], phi_ref[...], (1, 1))
    powers = jnp.exp(logits - jnp.max(logits, axis=1, keepdims=True))
    combine = powers * (1.0 / jnp.sum(powers, axis=1, keepdims=True))
    combine_b = combine.astype(BF16)
    mixed = sum(
        jnp.dot(combine_b[:, k * width : (k + 1) * width], o[...], preferred_element_type=F32)
        for k, o in enumerate(outs)
    )
    mixed_ref[...] = jnp.where(live_ref[:, :1] > 0.0, mixed, 0.0).astype(BF16)
    grad = grad_ref[...]
    combine_grad = jnp.concatenate([matmul(grad, o[...], (1, 1)) for o in outs], axis=1)
    product = combine * combine_grad
    logit_ref[...] = (product - combine * jnp.sum(product, axis=1, keepdims=True)).astype(BF16)


def tokens_kernel(live_ref, logit_ref, tokens_ref, phi_ref, *refs):
    messages, grads, out_ref, zero_ref = refs[:4], refs[4:8], refs[8], refs[9]
    zero_ref[...] = jnp.zeros_like(zero_ref)
    width = grads[0].shape[0] - 16

    def joined(line, arrays):
        rows = [m[...].astype(F32)[line : line + 1] for m in arrays]
        return jnp.concatenate([sum(r[:, k * width : (k + 1) * width] for k in range(3)) for r in rows], axis=1)

    top, inverse = joined(12, messages), joined(13, messages)
    column = joined(0, [g.at[width:, :] for g in grads])
    tokens = tokens_ref[...]
    logits = matmul(tokens, phi_ref[...], (1, 1))
    weights = jnp.where(live_ref[:, :1] > 0.0, jnp.exp(logits - top), 0.0).astype(BF16)
    share = weights.astype(F32) * inverse
    dispatch_grad = jnp.concatenate([matmul(tokens, g[:width, :], (1, 1)) for g in grads], axis=1)
    logit_grad = logit_ref[...].astype(F32) + share * (dispatch_grad - column)
    total = jnp.dot(logit_grad.astype(BF16), phi_ref[...], preferred_element_type=F32)
    share_b = share.astype(BF16)
    for k, g in enumerate(grads):
        total += jnp.dot(share_b[:, k * width : (k + 1) * width], g[:width, :], preferred_element_type=F32)
    out_ref[...] = total.astype(BF16)


def sum_kernel(parts_ref, zero_ref, out_ref):
    out_ref[...] = jnp.sum(parts_ref[...].astype(F32), axis=0) + zero_ref[:, :1]


def per_device(tokens, halt_steps, phi, w_up, w_down, cotangent):
    clip_part = tokens[0]
    rows, features = clip_part.shape
    planes = lax.axis_size("x")
    experts = lax.axis_size("y") * lax.axis_size("z") * lax.axis_size("core")
    live_rows = (halt_steps[0] > LAYER_POS)[:, None]
    masked_grad = jnp.where(live_rows, cotangent[0], jnp.zeros((), BF16))
    live_rows = live_rows.astype(F32)
    live_wide = jnp.broadcast_to(live_rows, (rows, 128))

    def whole(array):
        return (array, array.shape, None)

    def made(kind, *shape):
        return (kind, shape, shape, None)

    ahead, behind = to_neighbours(clip_part)
    far = pass_on(ahead, behind)
    phi_groups = gather_phi(phi)
    own_slots = phi_groups.shape[1]
    per_expert = own_slots // experts
    phi_all = phi_groups.reshape(-1, features)
    slots = phi_all.shape[0]

    logits = matmul(clip_part, phi_all, (1, 1))
    top = jnp.max(logits, axis=-1, keepdims=True)
    norm = live_rows / jnp.sum(jnp.exp(logits - top), axis=-1, keepdims=True)
    message = jnp.stack([top, norm]).reshape(2, -1, 128)
    row_stats = jnp.concatenate(gather_x(message), axis=1).reshape(2, 1, -1)

    grad_pieces = [masked_grad] + gather_x(masked_grad * unit(far[0], far[1], row_stats[0]))[1:]
    pieces = [clip_part, ahead, *far, behind]
    clip_rows = planes * rows

    def rows_of(values):
        return values.reshape(experts, per_expert, -1)

    weights, own_combine, slot_in, normed, factor, inverse, slot_top = call(
        dispatch_kernel,
        1,
        [whole(phi_groups[0]), whole(row_stats[0]), whole(row_stats[1]), *map(whole, pieces)],
        [
            made(BF16, own_slots, clip_rows),
            made(BF16, own_slots, clip_rows),
            made(BF16, own_slots, features),
            made(F32, own_slots, features),
            made(F32, own_slots, 1),
            made(F32, own_slots, 1),
            made(F32, own_slots, 1),
        ],
        [pltpu.VMEM((own_slots, clip_rows), F32)],
    )
    expert_in = exchange(rows_of(slot_in), GROUP).reshape(-1, features)

    up_matrix, down_matrix = w_up[0], w_down[0]
    hid = up_matrix.shape[1]
    steps = 6
    tile = hid // steps
    expert_rows = expert_in.shape[0]
    block, wide = (expert_rows, features), (expert_rows, tile)
    up, down = (up_matrix, (features, tile), 1), (down_matrix, (tile, features), 0)
    total = [pltpu.VMEM(block, F32)]
    hidden, slope, output = call(
        forward_kernel,
        steps,
        [whole(expert_in), up, down],
        [(BF16, (expert_rows, hid), wide, 1), (BF16, (expert_rows, hid), wide, 1), made(BF16, *block)],
        total,
    )
    (slot_grad,) = call(
        slot_kernel, 1, [whole(own_combine), *map(whole, grad_pieces)], [made(BF16, own_slots, features)]
    )
    arrived = exchange(rows_of(jnp.concatenate([slot_grad, output], axis=1)), GROUP).reshape(own_slots, -1)

    pre_grad, normed_grad = call(
        backward_kernel,
        steps,
        [(arrived, block, (0, 0)), (slope, wide, 1), up, down],
        [(BF16, (expert_rows, hid), wide, 1), made(BF16, *block)],
        total,
    )
    back_grad = exchange(rows_of(normed_grad), GROUP).reshape(own_slots, features)
    (grad_down,) = call(
        product_kernel,
        steps,
        [(hidden, wide, 1), (arrived, block, (0, 0))],
        [(BF16, down_matrix.shape, down[1], 0)],
    )
    (grad_up,) = call(
        product_kernel,
        steps,
        [whole(expert_in), (pre_grad, wide, 1)],
        [(BF16, up_matrix.shape, up[1], 1)],
    )

    slot_combine_grad, message = call(
        slot_grad_kernel,
        1,
        [
            (arrived, block, (0, 1)),
            (normed_grad, (16, 128), None),
            *map(whole, (own_combine, slot_top, inverse)),
            *map(whole, grad_pieces),
        ],
        [made(F32, own_slots, clip_rows), made(BF16, own_slots + 16, features)],
        [pltpu.VMEM((16, features), F32)],
    )
    slot_outs = gather_x(message)
    tails = [(m, (16, features), (own_slots // 16, 0)) for m in slot_outs]

    mixed_grad, own_column = call(
        mixed_grad_kernel,
        1,
        [whole(back_grad), whole(normed), whole(factor), (grad_down, (16, 128), None)],
        [made(BF16, own_slots + 16, features), made(F32, own_slots, 1)],
    )
    all_grads = gather_x(mixed_grad)
    (part_phi,) = call(
        phi_kernel,
        1,
        [
            (mixed_grad, (own_slots, features), None),
            whole(own_combine),
            whole(slot_combine_grad),
            whole(weights),
            whole(inverse),
            whole(own_column),
            *tails,
            *map(whole, pieces),
        ],
        [made(BF16, own_slots, features)],
    )
    arrived_phi = exchange(rows_of(part_phi), GROUP)

    part = 256
    thin, lanes = (part, features), (part, 128)
    mixed, combine_logit_grad = call(
        combine_kernel,
        rows // part,
        [
            (live_wide, lanes, 0),
            (clip_part, thin, 0),
            (masked_grad, thin, 0),
            whole(phi_all),
            *[(m, (own_slots, features), None) for m in slot_outs],
        ],
        [(BF16, clip_part.shape, thin, 0), (BF16, (rows, slots), (part, slots), 0)],
    )
    grad_rows, zero = call(
        tokens_kernel,
        rows // part,
        [
            (live_wide, lanes, 0),
            (combine_logit_grad, (part, slots), 0),
            (clip_part, thin, 0),
            whole(phi_all),
            *tails,
            *map(whole, all_grads),
        ],
        [(BF16, clip_part.shape, thin, 0), made(F32, 8, 128)],
        work=5 * 10**9,
    )
    (grad_phi_t,) = call(
        sum_kernel, 1, [whole(arrived_phi), whole(zero)], [made(F32, *arrived_phi.shape[1:])]
    )
    return (mixed[None], grad_rows[None], grad_phi_t, grad_up[None], grad_down[None])


def solution(mesh):
    fine = Mesh(mesh.devices.reshape(4, 4, 4, 2), ("x", "y", "z", "core"))
    rows = P(GROUP, "x", None)
    blocks = P(("x",) + GROUP, None, None)
    return jax.shard_map(
        per_device,
        mesh=fine,
        in_specs=(rows, P(GROUP, "x"), P(None, GROUP), blocks, blocks, rows),
        out_specs=(rows, rows, P(("x",) + GROUP, None), blocks, blocks),
        check_vma=False,
    )
```

```python
import functools
import math

import jax
import jax.numpy as jnp
from jax import lax
from jax.experimental import pallas as pl
from jax.experimental.pallas import tpu as pltpu
from jax.sharding import Mesh, PartitionSpec as P

LAYER_POS = 1
EPS = 1e-06
LOW_LOGIT = -1e30

PLANE = ("y", "z")
GROUP = ("y", "z", "core")
F32 = jnp.float32
BF16 = jnp.bfloat16


def matmul(a, b, contract):
    return lax.dot_general(a, b, ((contract[:1], contract[1:]), ((), ())), preferred_element_type=F32)


def swap_cores(values):
    return lax.ppermute(values, "core", [(0, 1), (1, 0)])


def along_x(values, steps):
    n = lax.axis_size("x")
    return lax.ppermute(values, "x", [(i, (i + steps) % n) for i in range(n)])


def gather_x(values):
    return [values] + [along_x(values, -k) for k in range(1, lax.axis_size("x"))]


def to_neighbours(values):
    return along_x(values, -1), along_x(values, 1)


def exchange(values, axes):
    return lax.all_to_all(values, axes, 0, 0, tiled=True)


def roll_blocks(blocks, first):
    return lax.dynamic_slice_in_dim(jnp.concatenate([blocks, blocks[:-1]]), first, blocks.shape[0], 0)


def gather_phi(phi, one):
    rows = phi.T
    planes = lax.axis_size("x")
    chips = lax.axis_size("y") * lax.axis_size("z")
    mine = exchange(jnp.broadcast_to(rows[None], (chips,) + rows.shape), PLANE) * one
    other = swap_cores(mine)
    first = lax.axis_index("core") == 0
    both = jnp.stack([jnp.where(first, mine, other), jnp.where(first, other, mine)], axis=1)
    groups = both.reshape(planes, -1, rows.shape[1])
    return roll_blocks(groups, lax.axis_index("x"))


def gelu_parts(v):
    scale = math.sqrt(2.0 / math.pi)
    square = v * v
    t = jnp.tanh(scale * v * (1.0 + 0.044715 * square))
    half = 0.5 * (1.0 + t)
    slope = half + 0.5 * scale * v * (1.0 - t * t) * (1.0 + 3.0 * 0.044715 * square)
    return v * half, slope


def unit(*arrays):
    return sum(a[0, 0].astype(BF16) * 0 for a in arrays) + jnp.ones((), BF16)


LIMIT = 56 * 1024 * 1024


def call(kernel, steps, inputs, outputs, scratch=(), work=1000):
    def spec(block, where):
        if where is None:
            where = (0,) * len(block)
        if isinstance(where, tuple):
            return pl.BlockSpec(block, lambda i: where)
        return pl.BlockSpec(block, lambda i: tuple(i if d == where else 0 for d in range(len(block))))

    return pl.pallas_call(
        kernel,
        grid=(steps,),
        in_specs=[spec(block, where) for _, block, where in inputs],
        out_specs=[spec(block, where) for _, _, block, where in outputs],
        out_shape=[jax.ShapeDtypeStruct(shape, kind) for kind, shape, _, _ in outputs],
        scratch_shapes=list(scratch),
        compiler_params=pltpu.CompilerParams(vmem_limit_bytes=LIMIT),
        cost_estimate=pl.CostEstimate(flops=work, bytes_accessed=1000, transcendentals=0),
    )(*[array for array, _, _ in inputs])


def accumulate(total, part, out_ref):
    step = pl.program_id(0)

    @pl.when(step == 0)
    def _():
        total[...] = part

    @pl.when(step > 0)
    def _():
        total[...] += part

    @pl.when(step == pl.num_programs(0) - 1)
    def _():
        out_ref[...] = total[...].astype(BF16)


def forward_kernel(rows_ref, up_ref, down_ref, hidden_ref, slope_ref, out_ref, total):
    preact = jnp.dot(rows_ref[...], up_ref[...], preferred_element_type=F32)
    hidden, slope = gelu_parts(preact)
    hidden = hidden.astype(BF16)
    hidden_ref[...] = hidden
    slope_ref[...] = slope.astype(BF16)
    accumulate(total, jnp.dot(hidden, down_ref[...], preferred_element_type=F32), out_ref)


def backward_kernel(grad_ref, slope_ref, up_ref, down_ref, _, pre_ref, out_ref, total):
    pre_grad = (slope_ref[...].astype(F32) * matmul(grad_ref[...], down_ref[...], (1, 1))).astype(BF16)
    pre_ref[...] = pre_grad
    accumulate(total, matmul(pre_grad, up_ref[...], (1, 1)), out_ref)


def weights_kernel(rows_ref, grad_ref, hidden_ref, pre_ref, up_ref, down_ref):
    up_ref[...] = matmul(rows_ref[...], pre_ref[...], (0, 0)).astype(BF16)
    down_ref[...] = matmul(hidden_ref[...], grad_ref[...], (0, 0)).astype(BF16)


def dispatch_kernel(
    phi_ref, tops_ref, norms_ref, *refs
):
    pieces, outs = refs[:5], refs[5:]
    weights_ref, combine_ref, in_ref, normed_ref, factor_ref, inverse_ref, top_ref, logits = outs
    phi = phi_ref[...]
    spans, at = [], 0
    for p in pieces:
        spans.append(slice(at, at + p.shape[0]))
        at += p.shape[0]
    top = None
    for p, span in zip(pieces, spans):
        l = matmul(phi, p[...], (1, 1))
        logits[:, span] = l
        norms = norms_ref[:, span]
        combine_ref[:, span] = (jnp.exp(l - tops_ref[:, span]) * norms).astype(BF16)
        here = jnp.max(jnp.where(norms > 0.0, l, LOW_LOGIT), axis=1, keepdims=True)
        top = here if top is None else jnp.maximum(top, here)
    slot_total, mixed = 0.0, 0.0
    for p, span in zip(pieces, spans):
        w = jnp.where(norms_ref[:, span] > 0.0, jnp.exp(logits[:, span] - top), 0.0).astype(BF16)
        weights_ref[:, span] = w
        slot_total += jnp.sum(w.astype(F32), axis=1, keepdims=True)
        mixed += jnp.dot(w, p[...], preferred_element_type=F32)
    inverse = 1.0 / slot_total
    mixed = mixed * inverse
    factor = lax.rsqrt(jnp.mean(mixed * mixed, axis=1, keepdims=True) + EPS)
    normed = mixed * factor
    normed_ref[...] = normed
    in_ref[...] = normed.astype(BF16)
    factor_ref[...] = factor
    inverse_ref[...] = inverse
    top_ref[...] = top


def slot_kernel(combine_ref, output_ref, *refs):
    *pieces, out_ref = refs
    total, at = 0.0, 0
    for p in pieces:
        total += jnp.dot(combine_ref[:, at : at + p.shape[0]], p[...], preferred_element_type=F32)
        at += p.shape[0]
    width = total.shape[1]
    out_ref[:, :width] = total.astype(BF16)
    out_ref[:, width:] = output_ref[...]


def halves_kernel(ahead_ref, behind_ref, ahead_out_ref, behind_out_ref):
    ahead_out_ref[...] = ahead_ref[...]
    behind_out_ref[...] = behind_ref[...]


def mask_kernel(live_ref, grad_ref, *refs):
    refs[-1][...] = jnp.where(live_ref[:, :1] > 0.0, grad_ref[...].astype(F32), 0.0).astype(BF16)


def softmax_kernel(live_ref, tokens_ref, phi_ref, _, out_ref):
    logits = matmul(tokens_ref[...], phi_ref[...], (1, 1))
    powers = jnp.exp(logits - jnp.max(logits, axis=1, keepdims=True))
    scale = live_ref[:, :1] / jnp.sum(powers, axis=1, keepdims=True)
    out_ref[...] = (powers * scale).astype(BF16)


def row_sum_kernel(*refs):
    *messages, out_ref = refs
    width = out_ref.shape[1] // len(messages)
    messages = [m[...].astype(F32) for m in messages]
    for line in range(len(messages)):
        rows = 0.0
        for k, m in enumerate(messages):
            for j in range(3):
                i = 4 * j + (line - k) % 4
                rows += m[i : i + 1, :width]
        out_ref[:, line * width : (line + 1) * width] = rows


def split(values):
    parts = []
    for _ in range(3):
        part = values.astype(BF16).astype(F32)
        parts.append(part)
        values = values - part
    return parts


def as_row(column):
    return jnp.transpose(jnp.broadcast_to(column, (column.shape[0], 128)))[:1]


def slot_grad_kernel(out_ref, _, combine_ref, top_ref, inverse_ref, *refs):
    *pieces, combine_grad_ref, message_ref, lines = refs
    own, at = out_ref[...], 0
    slots = own.shape[0]
    message_ref[:slots, :] = own
    lines[...] = jnp.zeros_like(lines)
    width = pieces[0].shape[0]
    for p in pieces:
        span = slice(at, at + p.shape[0])
        grad = matmul(own, p[...], (1, 1))
        combine_grad_ref[:, span] = grad
        sums = jnp.sum(combine_ref[:, span].astype(F32) * grad, axis=0, keepdims=True)
        line, start = at // width, at % width
        for k, part in enumerate(split(sums)):
            lines[4 * k + line : 4 * k + line + 1, start : start + p.shape[0]] = part
        at += p.shape[0]
    for line, ref in ((12, top_ref), (13, inverse_ref)):
        for k, part in enumerate(split(as_row(ref[...]))):
            lines[line : line + 1, k * slots : (k + 1) * slots] = part
    message_ref[slots:, :] = lines[...].astype(BF16)


def mixed_grad_kernel(back_ref, normed_ref, factor_ref, _down, _up, out_ref, column_ref):
    back = back_ref[...].astype(F32)
    normed, factor = normed_ref[...], factor_ref[...]
    out = (factor * (back - normed * jnp.mean(back * normed, axis=1, keepdims=True))).astype(BF16)
    slots = out.shape[0]
    out_ref[:slots, :] = out
    column = jnp.sum(normed * out.astype(F32), axis=1, keepdims=True) / factor
    column_ref[...] = column
    row = jnp.concatenate(split(as_row(column)), axis=1)
    out_ref[slots:, :] = jnp.broadcast_to(row, (16, row.shape[1])).astype(BF16)


def phi_kernel(grad_ref, combine_ref, combine_grad_ref, row_ref, weights_ref, inverse_ref, column_ref, *refs):
    *pieces, out_ref = refs
    grad = grad_ref[...]
    total, at = 0.0, 0
    for p in pieces:
        span = slice(at, at + p.shape[0])
        at += p.shape[0]
        rows = row_ref[:, span]
        tokens = p[...]
        share = weights_ref[:, span].astype(F32) * inverse_ref[...]
        logit_grad = combine_ref[:, span].astype(F32) * (combine_grad_ref[:, span] - rows) + share * (
            matmul(grad, tokens, (1, 1)) - column_ref[...]
        )
        total += jnp.dot(logit_grad.astype(BF16), tokens, preferred_element_type=F32)
    out_ref[...] = total.astype(BF16)


def combine_kernel(combine_ref, grad_ref, *refs):
    *outs, mixed_ref, logit_ref = refs
    width = outs[0].shape[0]
    combine_b = combine_ref[...]
    mixed = sum(
        jnp.dot(combine_b[:, k * width : (k + 1) * width], o[...], preferred_element_type=F32)
        for k, o in enumerate(outs)
    )
    mixed_ref[...] = mixed.astype(BF16)
    grad = grad_ref[...]
    combine_grad = jnp.concatenate([matmul(grad, o[...], (1, 1)) for o in outs], axis=1)
    combine = combine_b.astype(F32)
    product = combine * combine_grad
    logit_ref[...] = (product - combine * jnp.sum(product, axis=1, keepdims=True)).astype(BF16)


def tokens_kernel(live_ref, logit_ref, tokens_ref, phi_ref, *refs):
    messages, grads, out_ref, zero_ref = refs[:4], refs[4:8], refs[8], refs[9]
    zero_ref[...] = jnp.zeros_like(zero_ref)
    width = grads[0].shape[0] - 16

    def joined(line, arrays):
        rows = [m[...].astype(F32)[line : line + 1] for m in arrays]
        return jnp.concatenate([sum(r[:, k * width : (k + 1) * width] for k in range(3)) for r in rows], axis=1)

    top, inverse = joined(12, messages), joined(13, messages)
    column = joined(0, [g.at[width:, :] for g in grads])
    tokens = tokens_ref[...]
    logits = matmul(tokens, phi_ref[...], (1, 1))
    weights = jnp.where(live_ref[:, :1] > 0.0, jnp.exp(logits - top), 0.0).astype(BF16)
    share = weights.astype(F32) * inverse
    dispatch_grad = jnp.concatenate([matmul(tokens, g[:width, :], (1, 1)) for g in grads], axis=1)
    logit_grad = logit_ref[...].astype(F32) + share * (dispatch_grad - column)
    total = jnp.dot(logit_grad.astype(BF16), phi_ref[...], preferred_element_type=F32)
    share_b = share.astype(BF16)
    for k, g in enumerate(grads):
        total += jnp.dot(share_b[:, k * width : (k + 1) * width], g[:width, :], preferred_element_type=F32)
    out_ref[...] = total.astype(BF16)


def sum_kernel(parts_ref, zero_ref, out_ref):
    out_ref[...] = jnp.sum(parts_ref[...].astype(F32), axis=0) + zero_ref[:, :1]


def whole(array):
    return (array, array.shape, None)


def made(kind, *shape):
    return (kind, shape, shape, None)


def per_device(tokens, halt_steps, phi, w_up, w_down, cotangent):
    clip_part = tokens[0]
    rows, features = clip_part.shape
    planes = lax.axis_size("x")
    experts = lax.axis_size("y") * lax.axis_size("z") * lax.axis_size("core")
    live_rows = (halt_steps[0] > LAYER_POS)[:, None].astype(F32)
    live_wide = jnp.broadcast_to(live_rows, (rows, 128))

    ahead, behind = to_neighbours(clip_part)
    half = (rows // 2, features)
    ahead_half, behind_half = call(
        halves_kernel, 1, [(ahead, half, (1, 0)), (behind, half, (0, 0))], [made(BF16, *half)] * 2, work=10**10
    )
    far = along_x(behind_half, 1), along_x(ahead_half, -1)
    phi_groups = gather_phi(phi, unit(ahead_half))
    own_slots = phi_groups.shape[1]
    per_expert = own_slots // experts
    phi_all = phi_groups.reshape(-1, features)
    slots = phi_all.shape[0]

    logits = matmul(clip_part, phi_all, (1, 1))
    top = jnp.max(logits, axis=-1, keepdims=True)
    norm = live_rows / jnp.sum(jnp.exp(logits - top), axis=-1, keepdims=True)
    message = jnp.stack([top, norm]).reshape(2, -1, 128)
    row_stats = jnp.concatenate(gather_x(message), axis=1).reshape(2, 1, -1)

    (masked_grad,) = call(
        mask_kernel,
        1,
        [whole(live_wide), whole(cotangent[0])]
        + [(f, (16, 128), None) for f in far]
        + [(message, (2, 4, 128), None)],
        [made(BF16, rows, features)],
    )
    grad_pieces = gather_x(masked_grad)
    pieces = [clip_part, ahead, *far, behind]
    clip_rows = planes * rows

    def rows_of(values):
        return values.reshape(experts, per_expert, -1)

    weights, own_combine, slot_in, normed, factor, inverse, slot_top = call(
        dispatch_kernel,
        1,
        [whole(phi_groups[0]), whole(row_stats[0]), whole(row_stats[1]), *map(whole, pieces)],
        [
            made(BF16, own_slots, clip_rows),
            made(BF16, own_slots, clip_rows),
            made(BF16, own_slots, features),
            made(F32, own_slots, features),
            made(F32, own_slots, 1),
            made(F32, own_slots, 1),
            made(F32, own_slots, 1),
        ],
        [pltpu.VMEM((own_slots, clip_rows), F32)],
    )
    expert_in = exchange(rows_of(slot_in), GROUP).reshape(-1, features)

    up_matrix, down_matrix = w_up[0], w_down[0]
    hid = up_matrix.shape[1]
    steps = 4
    tile = hid // steps
    expert_rows = expert_in.shape[0]
    block, wide = (expert_rows, features), (expert_rows, tile)
    up, down = (up_matrix, (features, tile), 1), (down_matrix, (tile, features), 0)
    total = [pltpu.VMEM(block, F32)]
    hidden, slope, output = call(
        forward_kernel,
        steps,
        [whole(expert_in), up, down],
        [(BF16, (expert_rows, hid), wide, 1), (BF16, (expert_rows, hid), wide, 1), made(BF16, *block)],
        total,
    )
    (message,) = call(
        slot_kernel,
        1,
        [whole(own_combine), whole(output), *map(whole, grad_pieces)],
        [made(BF16, own_slots, 2 * features)],
    )
    arrived = exchange(rows_of(message), GROUP).reshape(own_slots, -1)
    part = 256
    thin, lanes = (part, features), (part, 128)
    (combine,) = call(
        softmax_kernel,
        rows // part,
        [(live_wide, lanes, 0), (clip_part, thin, 0), whole(phi_all), (output, (16, 128), None)],
        [(BF16, (rows, slots), (part, slots), 0)],
    )

    slot_combine_grad, message = call(
        slot_grad_kernel,
        1,
        [
            (arrived, block, (0, 1)),
            (combine, (16, 128), None),
            *map(whole, (own_combine, slot_top, inverse)),
            *map(whole, grad_pieces),
        ],
        [made(F32, own_slots, clip_rows), made(BF16, own_slots + 16, features)],
        [pltpu.VMEM((16, features), F32)],
    )
    slot_outs = gather_x(message)
    tails = [(m, (16, features), (own_slots // 16, 0)) for m in slot_outs]

    pre_grad, normed_grad = call(
        backward_kernel,
        steps,
        [
            (arrived, block, (0, 0)),
            (slope, wide, 1),
            up,
            down,
            (message, (16, 128), None),
        ],
        [(BF16, (expert_rows, hid), wide, 1), made(BF16, *block)],
        total,
    )
    back_grad = exchange(rows_of(normed_grad), GROUP).reshape(own_slots, features)
    grad_up, grad_down = call(
        weights_kernel,
        steps,
        [whole(expert_in), (arrived, block, (0, 0)), (hidden, wide, 1), (pre_grad, wide, 1)],
        [(BF16, up_matrix.shape, up[1], 1), (BF16, down_matrix.shape, down[1], 0)],
    )

    (row_sums,) = call(row_sum_kernel, 1, tails, [made(F32, 1, clip_rows)], work=2 * 10**10)

    mixed_grad, own_column = call(
        mixed_grad_kernel,
        1,
        [
            whole(back_grad),
            whole(normed),
            whole(factor),
            (grad_down, (16, 128), None),
            (grad_up, (16, 128), None),
        ],
        [made(BF16, own_slots + 16, features), made(F32, own_slots, 1)],
    )
    all_grads = gather_x(mixed_grad)
    (part_phi,) = call(
        phi_kernel,
        1,
        [
            (mixed_grad, (own_slots, features), None),
            whole(own_combine),
            whole(slot_combine_grad),
            whole(row_sums),
            whole(weights),
            whole(inverse),
            whole(own_column),
            *map(whole, pieces),
        ],
        [made(BF16, own_slots, features)],
    )
    arrived_phi = exchange(rows_of(part_phi), GROUP)

    mixed, combine_logit_grad = call(
        combine_kernel,
        rows // part,
        [
            (combine, (part, slots), 0),
            (masked_grad, thin, 0),
            *[(m, (own_slots, features), None) for m in slot_outs],
        ],
        [(BF16, clip_part.shape, thin, 0), (BF16, (rows, slots), (part, slots), 0)],
    )
    grad_rows, zero = call(
        tokens_kernel,
        rows // part,
        [
            (live_wide, lanes, 0),
            (combine_logit_grad, (part, slots), 0),
            (clip_part, thin, 0),
            whole(phi_all),
            *tails,
            *map(whole, all_grads),
        ],
        [(BF16, clip_part.shape, thin, 0), made(F32, 8, 128)],
        work=5 * 10**9,
    )
    (grad_phi_t,) = call(
        sum_kernel, 1, [whole(arrived_phi), whole(zero)], [made(F32, *arrived_phi.shape[1:])]
    )
    return (mixed[None], grad_rows[None], grad_phi_t, grad_up[None], grad_down[None])


def solution(mesh):
    fine = Mesh(mesh.devices.reshape(4, 4, 4, 2), ("x", "y", "z", "core"))
    rows = P(GROUP, "x", None)
    blocks = P(("x",) + GROUP, None, None)
    return jax.shard_map(
        per_device,
        mesh=fine,
        in_specs=(rows, P(GROUP, "x"), P(None, GROUP), blocks, blocks, rows),
        out_specs=(rows, rows, P(("x",) + GROUP, None), blocks, blocks),
        check_vma=False,
    )
```

```python
import functools
import math

import jax
import jax.numpy as jnp
from jax import lax
from jax.experimental import pallas as pl
from jax.experimental.pallas import tpu as pltpu
from jax.sharding import Mesh, PartitionSpec as P

LAYER_POS = 1
EPS = 1e-06
LOW_LOGIT = -1e30

PLANE = ("y", "z")
GROUP = ("y", "z", "core")
F32 = jnp.float32
BF16 = jnp.bfloat16


def matmul(a, b, contract):
    return lax.dot_general(a, b, ((contract[:1], contract[1:]), ((), ())), preferred_element_type=F32)


def swap_cores(values):
    return lax.ppermute(values, "core", [(0, 1), (1, 0)])


def along_x(values, steps):
    n = lax.axis_size("x")
    return lax.ppermute(values, "x", [(i, (i + steps) % n) for i in range(n)])


def gather_x(values):
    return [values] + [along_x(values, -k) for k in range(1, lax.axis_size("x"))]


def to_neighbours(values):
    return along_x(values, -1), along_x(values, 1)


def exchange(values, axes):
    return lax.all_to_all(values, axes, 0, 0, tiled=True)


def roll_blocks(blocks, first):
    return lax.dynamic_slice_in_dim(jnp.concatenate([blocks, blocks[:-1]]), first, blocks.shape[0], 0)


def gather_phi(phi, one):
    rows = phi.T
    planes = lax.axis_size("x")
    chips = lax.axis_size("y") * lax.axis_size("z")
    mine = exchange(jnp.broadcast_to(rows[None], (chips,) + rows.shape), PLANE) * one
    other = swap_cores(mine)
    first = lax.axis_index("core") == 0
    both = jnp.stack([jnp.where(first, mine, other), jnp.where(first, other, mine)], axis=1)
    groups = both.reshape(planes, -1, rows.shape[1])
    return roll_blocks(groups, lax.axis_index("x"))


def gelu_parts(v):
    scale = math.sqrt(2.0 / math.pi)
    square = v * v
    t = jnp.tanh(scale * v * (1.0 + 0.044715 * square))
    half = 0.5 * (1.0 + t)
    slope = half + 0.5 * scale * v * (1.0 - t * t) * (1.0 + 3.0 * 0.044715 * square)
    return v * half, slope


def unit(*arrays):
    return sum(a[0, 0].astype(BF16) * 0 for a in arrays) + jnp.ones((), BF16)


LIMIT = 56 * 1024 * 1024


def call(kernel, steps, inputs, outputs, scratch=(), work=1000):
    def spec(block, where):
        if where is None:
            where = (0,) * len(block)
        if isinstance(where, tuple):
            return pl.BlockSpec(block, lambda i: where)
        return pl.BlockSpec(block, lambda i: tuple(i if d == where else 0 for d in range(len(block))))

    return pl.pallas_call(
        kernel,
        grid=(steps,),
        in_specs=[spec(block, where) for _, block, where in inputs],
        out_specs=[spec(block, where) for _, _, block, where in outputs],
        out_shape=[jax.ShapeDtypeStruct(shape, kind) for kind, shape, _, _ in outputs],
        scratch_shapes=list(scratch),
        compiler_params=pltpu.CompilerParams(vmem_limit_bytes=LIMIT),
        cost_estimate=pl.CostEstimate(flops=work, bytes_accessed=1000, transcendentals=0),
    )(*[array for array, _, _ in inputs])


def accumulate(total, part, out_ref):
    step = pl.program_id(0)

    @pl.when(step == 0)
    def _():
        total[...] = part

    @pl.when(step > 0)
    def _():
        total[...] += part

    @pl.when(step == pl.num_programs(0) - 1)
    def _():
        out_ref[...] = total[...].astype(BF16)


def forward_kernel(rows_ref, up_ref, down_ref, hidden_ref, slope_ref, out_ref, total):
    preact = jnp.dot(rows_ref[...], up_ref[...], preferred_element_type=F32)
    hidden, slope = gelu_parts(preact)
    hidden = hidden.astype(BF16)
    hidden_ref[...] = hidden
    slope_ref[...] = slope.astype(BF16)
    accumulate(total, jnp.dot(hidden, down_ref[...], preferred_element_type=F32), out_ref)


def backward_kernel(grad_ref, slope_ref, up_ref, down_ref, _, pre_ref, out_ref, total):
    pre_grad = (slope_ref[...].astype(F32) * matmul(grad_ref[...], down_ref[...], (1, 1))).astype(BF16)
    pre_ref[...] = pre_grad
    accumulate(total, matmul(pre_grad, up_ref[...], (1, 1)), out_ref)


def weights_kernel(rows_ref, grad_ref, hidden_ref, pre_ref, up_ref, down_ref):
    up_ref[...] = matmul(rows_ref[...], pre_ref[...], (0, 0)).astype(BF16)
    down_ref[...] = matmul(hidden_ref[...], grad_ref[...], (0, 0)).astype(BF16)


def dispatch_kernel(
    phi_ref, tops_ref, norms_ref, *refs
):
    pieces, outs = refs[:5], refs[5:]
    weights_ref, combine_ref, in_ref, normed_ref, factor_ref, inverse_ref, top_ref, logits = outs
    phi = phi_ref[...]
    spans, at = [], 0
    for p in pieces:
        spans.append(slice(at, at + p.shape[0]))
        at += p.shape[0]
    top = None
    for p, span in zip(pieces, spans):
        l = matmul(phi, p[...], (1, 1))
        logits[:, span] = l
        norms = norms_ref[:, span]
        combine_ref[:, span] = (jnp.exp(l - tops_ref[:, span]) * norms).astype(BF16)
        here = jnp.max(jnp.where(norms > 0.0, l, LOW_LOGIT), axis=1, keepdims=True)
        top = here if top is None else jnp.maximum(top, here)
    slot_total, mixed = 0.0, 0.0
    for p, span in zip(pieces, spans):
        w = jnp.where(norms_ref[:, span] > 0.0, jnp.exp(logits[:, span] - top), 0.0).astype(BF16)
        weights_ref[:, span] = w
        slot_total += jnp.sum(w.astype(F32), axis=1, keepdims=True)
        mixed += jnp.dot(w, p[...], preferred_element_type=F32)
    inverse = 1.0 / slot_total
    mixed = mixed * inverse
    factor = lax.rsqrt(jnp.mean(mixed * mixed, axis=1, keepdims=True) + EPS)
    normed = mixed * factor
    normed_ref[...] = normed
    in_ref[...] = normed.astype(BF16)
    factor_ref[...] = factor
    inverse_ref[...] = inverse
    top_ref[...] = top


def slot_kernel(combine_ref, output_ref, *refs):
    *pieces, out_ref = refs
    total, at = 0.0, 0
    for p in pieces:
        total += jnp.dot(combine_ref[:, at : at + p.shape[0]], p[...], preferred_element_type=F32)
        at += p.shape[0]
    width = total.shape[1]
    out_ref[:, :width] = total.astype(BF16)
    out_ref[:, width:] = output_ref[...]


def halves_kernel(ahead_ref, behind_ref, _, ahead_out_ref, behind_out_ref):
    ahead_out_ref[...] = ahead_ref[...]
    behind_out_ref[...] = behind_ref[...]


def nothing_kernel(*refs):
    del refs


def tied(values, *others):
    where = pl.BlockSpec(memory_space=pl.ANY)
    return pl.pallas_call(
        nothing_kernel,
        in_specs=[where] * (1 + len(others)),
        out_specs=where,
        out_shape=jax.ShapeDtypeStruct(values.shape, values.dtype),
        input_output_aliases={0: 0},
        compiler_params=pltpu.CompilerParams(vmem_limit_bytes=LIMIT),
        cost_estimate=pl.CostEstimate(flops=1000, bytes_accessed=1000, transcendentals=0),
    )(values, *others)


def softmax_kernel(live_ref, tokens_ref, phi_ref, _, out_ref):
    logits = matmul(tokens_ref[...], phi_ref[...], (1, 1))
    powers = jnp.exp(logits - jnp.max(logits, axis=1, keepdims=True))
    scale = live_ref[:, :1] / jnp.sum(powers, axis=1, keepdims=True)
    out_ref[...] = (powers * scale).astype(BF16)


def row_sum_kernel(*refs):
    *messages, out_ref = refs
    width = out_ref.shape[1] // len(messages)
    messages = [m[...].astype(F32) for m in messages]
    for line in range(len(messages)):
        rows = 0.0
        for k, m in enumerate(messages):
            for j in range(3):
                i = 4 * j + (line - k) % 4
                rows += m[i : i + 1, :width]
        out_ref[:, line * width : (line + 1) * width] = rows


def split(values):
    parts = []
    for _ in range(3):
        part = values.astype(BF16).astype(F32)
        parts.append(part)
        values = values - part
    return parts


def as_row(column):
    return jnp.transpose(jnp.broadcast_to(column, (column.shape[0], 128)))[:1]


def slot_grad_kernel(out_ref, _, combine_ref, top_ref, inverse_ref, *refs):
    *pieces, combine_grad_ref, message_ref, lines = refs
    own, at = out_ref[...], 0
    slots = own.shape[0]
    message_ref[:slots, :] = own
    lines[...] = jnp.zeros_like(lines)
    width = pieces[0].shape[0]
    for p in pieces:
        span = slice(at, at + p.shape[0])
        grad = matmul(own, p[...], (1, 1))
        combine_grad_ref[:, span] = grad
        sums = jnp.sum(combine_ref[:, span].astype(F32) * grad, axis=0, keepdims=True)
        line, start = at // width, at % width
        for k, part in enumerate(split(sums)):
            lines[4 * k + line : 4 * k + line + 1, start : start + p.shape[0]] = part
        at += p.shape[0]
    for line, ref in ((12, top_ref), (13, inverse_ref)):
        for k, part in enumerate(split(as_row(ref[...]))):
            lines[line : line + 1, k * slots : (k + 1) * slots] = part
    message_ref[slots:, :] = lines[...].astype(BF16)


def mixed_grad_kernel(back_ref, normed_ref, factor_ref, _down, _up, out_ref, column_ref):
    back = back_ref[...].astype(F32)
    normed, factor = normed_ref[...], factor_ref[...]
    out = (factor * (back - normed * jnp.mean(back * normed, axis=1, keepdims=True))).astype(BF16)
    slots = out.shape[0]
    out_ref[:slots, :] = out
    column = jnp.sum(normed * out.astype(F32), axis=1, keepdims=True) / factor
    column_ref[...] = column
    row = jnp.concatenate(split(as_row(column)), axis=1)
    out_ref[slots:, :] = jnp.broadcast_to(row, (16, row.shape[1])).astype(BF16)


def phi_kernel(grad_ref, combine_ref, combine_grad_ref, row_ref, weights_ref, inverse_ref, column_ref, *refs):
    *pieces, out_ref = refs
    grad = grad_ref[...]
    total, at = 0.0, 0
    for p in pieces:
        span = slice(at, at + p.shape[0])
        at += p.shape[0]
        rows = row_ref[:, span]
        tokens = p[...]
        share = weights_ref[:, span].astype(F32) * inverse_ref[...]
        logit_grad = combine_ref[:, span].astype(F32) * (combine_grad_ref[:, span] - rows) + share * (
            matmul(grad, tokens, (1, 1)) - column_ref[...]
        )
        total += jnp.dot(logit_grad.astype(BF16), tokens, preferred_element_type=F32)
    out_ref[...] = total.astype(BF16)


def combine_kernel(combine_ref, grad_ref, *refs):
    *outs, mixed_ref, logit_ref = refs
    width = outs[0].shape[0]
    combine_b = combine_ref[...]
    mixed = sum(
        jnp.dot(combine_b[:, k * width : (k + 1) * width], o[...], preferred_element_type=F32)
        for k, o in enumerate(outs)
    )
    mixed_ref[...] = mixed.astype(BF16)
    grad = grad_ref[...]
    combine_grad = jnp.concatenate([matmul(grad, o[...], (1, 1)) for o in outs], axis=1)
    combine = combine_b.astype(F32)
    product = combine * combine_grad
    logit_ref[...] = (product - combine * jnp.sum(product, axis=1, keepdims=True)).astype(BF16)


def tokens_kernel(live_ref, logit_ref, tokens_ref, phi_ref, *refs):
    messages, grads, out_ref, zero_ref = refs[:4], refs[4:8], refs[8], refs[9]
    zero_ref[...] = jnp.zeros_like(zero_ref)
    width = grads[0].shape[0] - 16

    def joined(line, arrays):
        rows = [m[...].astype(F32)[line : line + 1] for m in arrays]
        return jnp.concatenate([sum(r[:, k * width : (k + 1) * width] for k in range(3)) for r in rows], axis=1)

    top, inverse = joined(12, messages), joined(13, messages)
    column = joined(0, [g.at[width:, :] for g in grads])
    tokens = tokens_ref[...]
    logits = matmul(tokens, phi_ref[...], (1, 1))
    weights = jnp.where(live_ref[:, :1] > 0.0, jnp.exp(logits - top), 0.0).astype(BF16)
    share = weights.astype(F32) * inverse
    dispatch_grad = jnp.concatenate([matmul(tokens, g[:width, :], (1, 1)) for g in grads], axis=1)
    logit_grad = logit_ref[...].astype(F32) + share * (dispatch_grad - column)
    total = jnp.dot(logit_grad.astype(BF16), phi_ref[...], preferred_element_type=F32)
    share_b = share.astype(BF16)
    for k, g in enumerate(grads):
        total += jnp.dot(share_b[:, k * width : (k + 1) * width], g[:width, :], preferred_element_type=F32)
    out_ref[...] = total.astype(BF16)


def sum_kernel(parts_ref, zero_ref, out_ref):
    out_ref[...] = jnp.sum(parts_ref[...].astype(F32), axis=0) + zero_ref[:, :1]


def whole(array):
    return (array, array.shape, None)


def made(kind, *shape):
    return (kind, shape, shape, None)


def per_device(tokens, halt_steps, phi, w_up, w_down, cotangent):
    clip_part = tokens[0]
    rows, features = clip_part.shape
    planes = lax.axis_size("x")
    experts = lax.axis_size("y") * lax.axis_size("z") * lax.axis_size("core")
    live_rows = (halt_steps[0] > LAYER_POS)[:, None]
    masked_grad = jnp.where(live_rows, cotangent[0], jnp.zeros((), BF16))
    live_rows = live_rows.astype(F32)
    live_wide = jnp.broadcast_to(live_rows, (rows, 128))

    ahead, behind = to_neighbours(clip_part)
    half = (rows // 2, features)
    ahead_half, behind_half = call(
        halves_kernel, 1, [(ahead, half, (1, 0)), (behind, half, (0, 0)), (masked_grad, (16, 128), None)], [made(BF16, *half)] * 2,
        work=10**10,
    )
    far = along_x(behind_half, 1), along_x(ahead_half, -1)
    phi_groups = gather_phi(phi, unit(ahead_half))
    own_slots = phi_groups.shape[1]
    per_expert = own_slots // experts
    phi_all = phi_groups.reshape(-1, features)
    slots = phi_all.shape[0]

    logits = matmul(clip_part, phi_all, (1, 1))
    top = jnp.max(logits, axis=-1, keepdims=True)
    norm = live_rows / jnp.sum(jnp.exp(logits - top), axis=-1, keepdims=True)
    message = jnp.stack([top, norm]).reshape(2, -1, 128)
    row_stats = jnp.concatenate(gather_x(message), axis=1).reshape(2, 1, -1)

    masked_grad = tied(masked_grad, *far, message)
    grad_pieces = gather_x(masked_grad)
    pieces = [clip_part, ahead, *far, behind]
    clip_rows = planes * rows

    def rows_of(values):
        return values.reshape(experts, per_expert, -1)

    weights, own_combine, slot_in, normed, factor, inverse, slot_top = call(
        dispatch_kernel,
        1,
        [whole(phi_groups[0]), whole(row_stats[0]), whole(row_stats[1]), *map(whole, pieces)],
        [
            made(BF16, own_slots, clip_rows),
            made(BF16, own_slots, clip_rows),
            made(BF16, own_slots, features),
            made(F32, own_slots, features),
            made(F32, own_slots, 1),
            made(F32, own_slots, 1),
            made(F32, own_slots, 1),
        ],
        [pltpu.VMEM((own_slots, clip_rows), F32)],
    )
    expert_in = exchange(rows_of(slot_in), GROUP).reshape(-1, features)

    up_matrix, down_matrix = w_up[0], w_down[0]
    hid = up_matrix.shape[1]
    steps = 4
    tile = hid // steps
    expert_rows = expert_in.shape[0]
    block, wide = (expert_rows, features), (expert_rows, tile)
    up, down = (up_matrix, (features, tile), 1), (down_matrix, (tile, features), 0)
    total = [pltpu.VMEM(block, F32)]
    hidden, slope, output = call(
        forward_kernel,
        steps,
        [whole(expert_in), up, down],
        [(BF16, (expert_rows, hid), wide, 1), (BF16, (expert_rows, hid), wide, 1), made(BF16, *block)],
        total,
    )
    (message,) = call(
        slot_kernel,
        1,
        [whole(own_combine), whole(output), *map(whole, grad_pieces)],
        [made(BF16, own_slots, 2 * features)],
    )
    arrived = exchange(rows_of(message), GROUP).reshape(own_slots, -1)
    part = 256
    thin, lanes = (part, features), (part, 128)
    (combine,) = call(
        softmax_kernel,
        rows // part,
        [(live_wide, lanes, 0), (clip_part, thin, 0), whole(phi_all), (output, (16, 128), None)],
        [(BF16, (rows, slots), (part, slots), 0)],
    )

    slot_combine_grad, message = call(
        slot_grad_kernel,
        1,
        [
            (arrived, block, (0, 1)),
            (combine, (16, 128), None),
            *map(whole, (own_combine, slot_top, inverse)),
            *map(whole, grad_pieces),
        ],
        [made(F32, own_slots, clip_rows), made(BF16, own_slots + 16, features)],
        [pltpu.VMEM((16, features), F32)],
    )
    slot_outs = gather_x(message)
    tails = [(m, (16, features), (own_slots // 16, 0)) for m in slot_outs]

    pre_grad, normed_grad = call(
        backward_kernel,
        steps,
        [
            (arrived, block, (0, 0)),
            (slope, wide, 1),
            up,
            down,
            (message, (16, 128), None),
        ],
        [(BF16, (expert_rows, hid), wide, 1), made(BF16, *block)],
        total,
    )
    back_grad = exchange(rows_of(normed_grad), GROUP).reshape(own_slots, features)
    grad_up, grad_down = call(
        weights_kernel,
        steps,
        [whole(expert_in), (arrived, block, (0, 0)), (hidden, wide, 1), (pre_grad, wide, 1)],
        [(BF16, up_matrix.shape, up[1], 1), (BF16, down_matrix.shape, down[1], 0)],
    )

    (row_sums,) = call(row_sum_kernel, 1, tails, [made(F32, 1, clip_rows)], work=2 * 10**10)

    mixed_grad, own_column = call(
        mixed_grad_kernel,
        1,
        [
            whole(back_grad),
            whole(normed),
            whole(factor),
            (grad_down, (16, 128), None),
            (grad_up, (16, 128), None),
        ],
        [made(BF16, own_slots + 16, features), made(F32, own_slots, 1)],
    )
    all_grads = gather_x(mixed_grad)
    (part_phi,) = call(
        phi_kernel,
        1,
        [
            (mixed_grad, (own_slots, features), None),
            whole(own_combine),
            whole(slot_combine_grad),
            whole(row_sums),
            whole(weights),
            whole(inverse),
            whole(own_column),
            *map(whole, pieces),
        ],
        [made(BF16, own_slots, features)],
    )
    arrived_phi = exchange(rows_of(part_phi), GROUP)

    mixed, combine_logit_grad = call(
        combine_kernel,
        rows // part,
        [
            (combine, (part, slots), 0),
            (masked_grad, thin, 0),
            *[(m, (own_slots, features), None) for m in slot_outs],
        ],
        [(BF16, clip_part.shape, thin, 0), (BF16, (rows, slots), (part, slots), 0)],
    )
    grad_rows, zero = call(
        tokens_kernel,
        rows // part,
        [
            (live_wide, lanes, 0),
            (combine_logit_grad, (part, slots), 0),
            (clip_part, thin, 0),
            whole(phi_all),
            *tails,
            *map(whole, all_grads),
        ],
        [(BF16, clip_part.shape, thin, 0), made(F32, 8, 128)],
        work=5 * 10**9,
    )
    (grad_phi_t,) = call(
        sum_kernel, 1, [whole(arrived_phi), whole(zero)], [made(F32, *arrived_phi.shape[1:])]
    )
    return (mixed[None], grad_rows[None], grad_phi_t, grad_up[None], grad_down[None])


def solution(mesh):
    fine = Mesh(mesh.devices.reshape(4, 4, 4, 2), ("x", "y", "z", "core"))
    rows = P(GROUP, "x", None)
    blocks = P(("x",) + GROUP, None, None)
    return jax.shard_map(
        per_device,
        mesh=fine,
        in_specs=(rows, P(GROUP, "x"), P(None, GROUP), blocks, blocks, rows),
        out_specs=(rows, rows, P(("x",) + GROUP, None), blocks, blocks),
        check_vma=False,
    )
```

```python
import functools
import math

import jax
import jax.numpy as jnp
from jax import lax
from jax.experimental import pallas as pl
from jax.experimental.pallas import tpu as pltpu
from jax.sharding import Mesh, PartitionSpec as P

LAYER_POS = 1
EPS = 1e-06
LOW_LOGIT = -1e30

PLANE = ("y", "z")
GROUP = ("y", "z", "core")
F32 = jnp.float32
BF16 = jnp.bfloat16


def matmul(a, b, contract):
    return lax.dot_general(a, b, ((contract[:1], contract[1:]), ((), ())), preferred_element_type=F32)


def swap_cores(values):
    return lax.ppermute(values, "core", [(0, 1), (1, 0)])


def along_x(values, steps):
    n = lax.axis_size("x")
    return lax.ppermute(values, "x", [(i, (i + steps) % n) for i in range(n)])


def gather_x(values):
    return [values] + [along_x(values, -k) for k in range(1, lax.axis_size("x"))]


def to_neighbours(values):
    return along_x(values, -1), along_x(values, 1)


def exchange(values, axes):
    return lax.all_to_all(values, axes, 0, 0, tiled=True)


def roll_blocks(blocks, first):
    return lax.dynamic_slice_in_dim(jnp.concatenate([blocks, blocks[:-1]]), first, blocks.shape[0], 0)


def gather_phi(phi, ahead_half):
    rows = phi.T
    planes = lax.axis_size("x")
    chips = lax.axis_size("y") * lax.axis_size("z")
    mine = tied(exchange(jnp.broadcast_to(rows[None], (chips,) + rows.shape), PLANE), ahead_half)
    other = swap_cores(mine)
    first = lax.axis_index("core") == 0
    both = jnp.stack([jnp.where(first, mine, other), jnp.where(first, other, mine)], axis=1)
    groups = both.reshape(planes, -1, rows.shape[1])
    return roll_blocks(groups, lax.axis_index("x"))


def gelu_parts(v):
    scale = math.sqrt(2.0 / math.pi)
    square = v * v
    t = jnp.tanh(scale * v * (1.0 + 0.044715 * square))
    half = 0.5 * (1.0 + t)
    slope = half + 0.5 * scale * v * (1.0 - t * t) * (1.0 + 3.0 * 0.044715 * square)
    return v * half, slope


LIMIT = 56 * 1024 * 1024


def call(kernel, steps, inputs, outputs, scratch=(), work=1000):
    def spec(block, where):
        if where is None:
            where = (0,) * len(block)
        if isinstance(where, tuple):
            return pl.BlockSpec(block, lambda i: where)
        return pl.BlockSpec(block, lambda i: tuple(i if d == where else 0 for d in range(len(block))))

    return pl.pallas_call(
        kernel,
        grid=(steps,),
        in_specs=[spec(block, where) for _, block, where in inputs],
        out_specs=[spec(block, where) for _, _, block, where in outputs],
        out_shape=[jax.ShapeDtypeStruct(shape, kind) for kind, shape, _, _ in outputs],
        scratch_shapes=list(scratch),
        compiler_params=pltpu.CompilerParams(vmem_limit_bytes=LIMIT),
        cost_estimate=pl.CostEstimate(flops=work, bytes_accessed=1000, transcendentals=0),
    )(*[array for array, _, _ in inputs])


def accumulate(total, part, out_ref):
    step = pl.program_id(0)

    @pl.when(step == 0)
    def _():
        total[...] = part

    @pl.when(step > 0)
    def _():
        total[...] += part

    @pl.when(step == pl.num_programs(0) - 1)
    def _():
        out_ref[...] = total[...].astype(BF16)


def forward_kernel(rows_ref, up_ref, down_ref, hidden_ref, slope_ref, out_ref, total):
    preact = jnp.dot(rows_ref[...], up_ref[...], preferred_element_type=F32)
    hidden, slope = gelu_parts(preact)
    hidden = hidden.astype(BF16)
    hidden_ref[...] = hidden
    slope_ref[...] = slope.astype(BF16)
    accumulate(total, jnp.dot(hidden, down_ref[...], preferred_element_type=F32), out_ref)


def backward_kernel(grad_ref, slope_ref, up_ref, down_ref, _, pre_ref, out_ref, total):
    pre_grad = (slope_ref[...].astype(F32) * matmul(grad_ref[...], down_ref[...], (1, 1))).astype(BF16)
    pre_ref[...] = pre_grad
    accumulate(total, matmul(pre_grad, up_ref[...], (1, 1)), out_ref)


def weights_kernel(rows_ref, grad_ref, hidden_ref, pre_ref, up_ref, down_ref):
    up_ref[...] = matmul(rows_ref[...], pre_ref[...], (0, 0)).astype(BF16)
    down_ref[...] = matmul(hidden_ref[...], grad_ref[...], (0, 0)).astype(BF16)


def dispatch_kernel(
    phi_ref, tops_ref, norms_ref, *refs
):
    pieces, outs = refs[:5], refs[5:]
    weights_ref, combine_ref, in_ref, normed_ref, factor_ref, inverse_ref, top_ref, logits = outs
    phi = phi_ref[...]
    spans, at = [], 0
    for p in pieces:
        spans.append(slice(at, at + p.shape[0]))
        at += p.shape[0]
    top = None
    for p, span in zip(pieces, spans):
        l = matmul(phi, p[...], (1, 1))
        logits[:, span] = l
        norms = norms_ref[:, span]
        combine_ref[:, span] = (jnp.exp(l - tops_ref[:, span]) * norms).astype(BF16)
        here = jnp.max(jnp.where(norms > 0.0, l, LOW_LOGIT), axis=1, keepdims=True)
        top = here if top is None else jnp.maximum(top, here)
    slot_total, mixed = 0.0, 0.0
    for p, span in zip(pieces, spans):
        w = jnp.where(norms_ref[:, span] > 0.0, jnp.exp(logits[:, span] - top), 0.0).astype(BF16)
        weights_ref[:, span] = w
        slot_total += jnp.sum(w.astype(F32), axis=1, keepdims=True)
        mixed += jnp.dot(w, p[...], preferred_element_type=F32)
    inverse = 1.0 / slot_total
    mixed = mixed * inverse
    factor = lax.rsqrt(jnp.mean(mixed * mixed, axis=1, keepdims=True) + EPS)
    normed = mixed * factor
    normed_ref[...] = normed
    in_ref[...] = normed.astype(BF16)
    factor_ref[...] = factor
    inverse_ref[...] = inverse
    top_ref[...] = top


def slot_kernel(combine_ref, output_ref, *refs):
    *pieces, out_ref = refs
    total, at = 0.0, 0
    for p in pieces:
        total += jnp.dot(combine_ref[:, at : at + p.shape[0]], p[...], preferred_element_type=F32)
        at += p.shape[0]
    width = total.shape[1]
    out_ref[:, :width] = total.astype(BF16)
    out_ref[:, width:] = output_ref[...]


def halves_kernel(ahead_ref, behind_ref, _, ahead_out_ref, behind_out_ref):
    ahead_out_ref[...] = ahead_ref[...]
    behind_out_ref[...] = behind_ref[...]


def nothing_kernel(*refs):
    del refs


def tied(values, *others):
    where = pl.BlockSpec(memory_space=pl.ANY)
    return pl.pallas_call(
        nothing_kernel,
        in_specs=[where] * (1 + len(others)),
        out_specs=where,
        out_shape=jax.ShapeDtypeStruct(values.shape, values.dtype),
        input_output_aliases={0: 0},
        compiler_params=pltpu.CompilerParams(vmem_limit_bytes=LIMIT),
        cost_estimate=pl.CostEstimate(flops=1000, bytes_accessed=1000, transcendentals=0),
    )(values, *others)


def softmax_kernel(live_ref, tokens_ref, phi_ref, _, out_ref):
    logits = matmul(tokens_ref[...], phi_ref[...], (1, 1))
    powers = jnp.exp(logits - jnp.max(logits, axis=1, keepdims=True))
    scale = live_ref[:, :1] / jnp.sum(powers, axis=1, keepdims=True)
    out_ref[...] = (powers * scale).astype(BF16)


def row_sum_kernel(*refs):
    *messages, out_ref = refs
    width = out_ref.shape[1] // len(messages)
    messages = [m[...].astype(F32) for m in messages]
    for line in range(len(messages)):
        rows = 0.0
        for k, m in enumerate(messages):
            for j in range(3):
                i = 4 * j + (line - k) % 4
                rows += m[i : i + 1, :width]
        out_ref[:, line * width : (line + 1) * width] = rows


def split(values):
    parts = []
    for _ in range(3):
        part = values.astype(BF16).astype(F32)
        parts.append(part)
        values = values - part
    return parts


def as_row(column):
    return jnp.transpose(jnp.broadcast_to(column, (column.shape[0], 128)))[:1]


def slot_grad_kernel(out_ref, _, combine_ref, top_ref, inverse_ref, *refs):
    *pieces, combine_grad_ref, message_ref, lines = refs
    own, at = out_ref[...], 0
    slots = own.shape[0]
    message_ref[:slots, :] = own
    lines[...] = jnp.zeros_like(lines)
    width = pieces[0].shape[0]
    for p in pieces:
        span = slice(at, at + p.shape[0])
        grad = matmul(own, p[...], (1, 1))
        combine_grad_ref[:, span] = grad
        sums = jnp.sum(combine_ref[:, span].astype(F32) * grad, axis=0, keepdims=True)
        line, start = at // width, at % width
        for k, part in enumerate(split(sums)):
            lines[4 * k + line : 4 * k + line + 1, start : start + p.shape[0]] = part
        at += p.shape[0]
    for line, ref in ((12, top_ref), (13, inverse_ref)):
        for k, part in enumerate(split(as_row(ref[...]))):
            lines[line : line + 1, k * slots : (k + 1) * slots] = part
    message_ref[slots:, :] = lines[...].astype(BF16)


def mixed_grad_kernel(back_ref, normed_ref, factor_ref, _down, _up, out_ref, column_ref):
    back = back_ref[...].astype(F32)
    normed, factor = normed_ref[...], factor_ref[...]
    out = (factor * (back - normed * jnp.mean(back * normed, axis=1, keepdims=True))).astype(BF16)
    slots = out.shape[0]
    out_ref[:slots, :] = out
    column = jnp.sum(normed * out.astype(F32), axis=1, keepdims=True) / factor
    column_ref[...] = column
    row = jnp.concatenate(split(as_row(column)), axis=1)
    out_ref[slots:, :] = jnp.broadcast_to(row, (16, row.shape[1])).astype(BF16)


def phi_kernel(grad_ref, combine_ref, combine_grad_ref, row_ref, weights_ref, inverse_ref, column_ref, *refs):
    *pieces, out_ref = refs
    grad = grad_ref[...]
    total, at = 0.0, 0
    for p in pieces:
        span = slice(at, at + p.shape[0])
        at += p.shape[0]
        rows = row_ref[:, span]
        tokens = p[...]
        share = weights_ref[:, span].astype(F32) * inverse_ref[...]
        logit_grad = combine_ref[:, span].astype(F32) * (combine_grad_ref[:, span] - rows) + share * (
            matmul(grad, tokens, (1, 1)) - column_ref[...]
        )
        total += jnp.dot(logit_grad.astype(BF16), tokens, preferred_element_type=F32)
    out_ref[...] = total.astype(BF16)


def combine_kernel(combine_ref, grad_ref, *refs):
    *outs, mixed_ref, logit_ref = refs
    width = outs[0].shape[0]
    combine_b = combine_ref[...]
    mixed = sum(
        jnp.dot(combine_b[:, k * width : (k + 1) * width], o[...], preferred_element_type=F32)
        for k, o in enumerate(outs)
    )
    mixed_ref[...] = mixed.astype(BF16)
    grad = grad_ref[...]
    combine_grad = jnp.concatenate([matmul(grad, o[...], (1, 1)) for o in outs], axis=1)
    combine = combine_b.astype(F32)
    product = combine * combine_grad
    logit_ref[...] = (product - combine * jnp.sum(product, axis=1, keepdims=True)).astype(BF16)


def tokens_kernel(live_ref, logit_ref, tokens_ref, phi_ref, *refs):
    messages, grads, out_ref, zero_ref = refs[:4], refs[4:8], refs[8], refs[9]
    zero_ref[...] = jnp.zeros_like(zero_ref)
    width = grads[0].shape[0] - 16

    def joined(line, arrays):
        rows = [m[...].astype(F32)[line : line + 1] for m in arrays]
        return jnp.concatenate([sum(r[:, k * width : (k + 1) * width] for k in range(3)) for r in rows], axis=1)

    top, inverse = joined(12, messages), joined(13, messages)
    column = joined(0, [g.at[width:, :] for g in grads])
    tokens = tokens_ref[...]
    logits = matmul(tokens, phi_ref[...], (1, 1))
    weights = jnp.where(live_ref[:, :1] > 0.0, jnp.exp(logits - top), 0.0).astype(BF16)
    share = weights.astype(F32) * inverse
    dispatch_grad = jnp.concatenate([matmul(tokens, g[:width, :], (1, 1)) for g in grads], axis=1)
    logit_grad = logit_ref[...].astype(F32) + share * (dispatch_grad - column)
    total = jnp.dot(logit_grad.astype(BF16), phi_ref[...], preferred_element_type=F32)
    share_b = share.astype(BF16)
    for k, g in enumerate(grads):
        total += jnp.dot(share_b[:, k * width : (k + 1) * width], g[:width, :], preferred_element_type=F32)
    out_ref[...] = total.astype(BF16)


def sum_kernel(parts_ref, zero_ref, out_ref):
    out_ref[...] = jnp.sum(parts_ref[...].astype(F32), axis=0) + zero_ref[:, :1]


def whole(array):
    return (array, array.shape, None)


def made(kind, *shape):
    return (kind, shape, shape, None)


def per_device(tokens, halt_steps, phi, w_up, w_down, cotangent):
    clip_part = tokens[0]
    rows, features = clip_part.shape
    planes = lax.axis_size("x")
    experts = lax.axis_size("y") * lax.axis_size("z") * lax.axis_size("core")
    live_rows = (halt_steps[0] > LAYER_POS)[:, None]
    masked_grad = jnp.where(live_rows, cotangent[0], jnp.zeros((), BF16))
    live_rows = live_rows.astype(F32)
    live_wide = jnp.broadcast_to(live_rows, (rows, 128))

    ahead, behind = to_neighbours(clip_part)
    half = (rows // 2, features)
    ahead_half, behind_half = call(
        halves_kernel, 1, [(ahead, half, (1, 0)), (behind, half, (0, 0)), (masked_grad, (16, 128), None)], [made(BF16, *half)] * 2,
        work=10**10,
    )
    far = along_x(behind_half, 1), along_x(ahead_half, -1)
    phi_groups = gather_phi(phi, ahead_half)
    own_slots = phi_groups.shape[1]
    per_expert = own_slots // experts
    phi_all = phi_groups.reshape(-1, features)
    slots = phi_all.shape[0]

    logits = matmul(clip_part, phi_all, (1, 1))
    top = jnp.max(logits, axis=-1, keepdims=True)
    norm = live_rows / jnp.sum(jnp.exp(logits - top), axis=-1, keepdims=True)
    message = jnp.stack([top, norm]).reshape(2, -1, 128)
    row_stats = jnp.concatenate(gather_x(message), axis=1).reshape(2, 1, -1)

    masked_grad = tied(masked_grad, *far, message)
    grad_pieces = gather_x(masked_grad)
    pieces = [clip_part, ahead, *far, behind]
    clip_rows = planes * rows

    def rows_of(values):
        return values.reshape(experts, per_expert, -1)

    weights, own_combine, slot_in, normed, factor, inverse, slot_top = call(
        dispatch_kernel,
        1,
        [whole(phi_groups[0]), whole(row_stats[0]), whole(row_stats[1]), *map(whole, pieces)],
        [
            made(BF16, own_slots, clip_rows),
            made(BF16, own_slots, clip_rows),
            made(BF16, own_slots, features),
            made(F32, own_slots, features),
            made(F32, own_slots, 1),
            made(F32, own_slots, 1),
            made(F32, own_slots, 1),
        ],
        [pltpu.VMEM((own_slots, clip_rows), F32)],
    )
    expert_in = exchange(rows_of(slot_in), GROUP).reshape(-1, features)

    up_matrix, down_matrix = w_up[0], w_down[0]
    hid = up_matrix.shape[1]
    steps = 4
    tile = hid // steps
    expert_rows = expert_in.shape[0]
    block, wide = (expert_rows, features), (expert_rows, tile)
    up, down = (up_matrix, (features, tile), 1), (down_matrix, (tile, features), 0)
    total = [pltpu.VMEM(block, F32)]
    hidden, slope, output = call(
        forward_kernel,
        steps,
        [whole(expert_in), up, down],
        [(BF16, (expert_rows, hid), wide, 1), (BF16, (expert_rows, hid), wide, 1), made(BF16, *block)],
        total,
    )
    (message,) = call(
        slot_kernel,
        1,
        [whole(own_combine), whole(output), *map(whole, grad_pieces)],
        [made(BF16, own_slots, 2 * features)],
    )
    arrived = exchange(rows_of(message), GROUP).reshape(own_slots, -1)
    part = 256
    thin, lanes = (part, features), (part, 128)
    (combine,) = call(
        softmax_kernel,
        rows // part,
        [(live_wide, lanes, 0), (clip_part, thin, 0), whole(phi_all), (output, (16, 128), None)],
        [(BF16, (rows, slots), (part, slots), 0)],
    )

    slot_combine_grad, message = call(
        slot_grad_kernel,
        1,
        [
            (arrived, block, (0, 1)),
            (combine, (16, 128), None),
            *map(whole, (own_combine, slot_top, inverse)),
            *map(whole, grad_pieces),
        ],
        [made(F32, own_slots, clip_rows), made(BF16, own_slots + 16, features)],
        [pltpu.VMEM((16, features), F32)],
    )
    slot_outs = gather_x(message)
    tails = [(m, (16, features), (own_slots // 16, 0)) for m in slot_outs]

    pre_grad, normed_grad = call(
        backward_kernel,
        steps,
        [
            (arrived, block, (0, 0)),
            (slope, wide, 1),
            up,
            down,
            (message, (16, 128), None),
        ],
        [(BF16, (expert_rows, hid), wide, 1), made(BF16, *block)],
        total,
    )
    back_grad = exchange(rows_of(normed_grad), GROUP).reshape(own_slots, features)
    grad_up, grad_down = call(
        weights_kernel,
        steps,
        [whole(expert_in), (arrived, block, (0, 0)), (hidden, wide, 1), (pre_grad, wide, 1)],
        [(BF16, up_matrix.shape, up[1], 1), (BF16, down_matrix.shape, down[1], 0)],
    )

    (row_sums,) = call(row_sum_kernel, 1, tails, [made(F32, 1, clip_rows)], work=2 * 10**10)

    mixed_grad, own_column = call(
        mixed_grad_kernel,
        1,
        [
            whole(back_grad),
            whole(normed),
            whole(factor),
            (grad_down, (16, 128), None),
            (grad_up, (16, 128), None),
        ],
        [made(BF16, own_slots + 16, features), made(F32, own_slots, 1)],
    )
    all_grads = gather_x(mixed_grad)
    (part_phi,) = call(
        phi_kernel,
        1,
        [
            (mixed_grad, (own_slots, features), None),
            whole(own_combine),
            whole(slot_combine_grad),
            whole(row_sums),
            whole(weights),
            whole(inverse),
            whole(own_column),
            *map(whole, pieces),
        ],
        [made(BF16, own_slots, features)],
    )
    arrived_phi = exchange(rows_of(part_phi), GROUP)

    mixed, combine_logit_grad = call(
        combine_kernel,
        rows // part,
        [
            (combine, (part, slots), 0),
            (masked_grad, thin, 0),
            *[(m, (own_slots, features), None) for m in slot_outs],
        ],
        [(BF16, clip_part.shape, thin, 0), (BF16, (rows, slots), (part, slots), 0)],
    )
    grad_rows, zero = call(
        tokens_kernel,
        rows // part,
        [
            (live_wide, lanes, 0),
            (combine_logit_grad, (part, slots), 0),
            (clip_part, thin, 0),
            whole(phi_all),
            *tails,
            *map(whole, all_grads),
        ],
        [(BF16, clip_part.shape, thin, 0), made(F32, 8, 128)],
        work=5 * 10**9,
    )
    (grad_phi_t,) = call(
        sum_kernel, 1, [whole(arrived_phi), whole(zero)], [made(F32, *arrived_phi.shape[1:])]
    )
    return (mixed[None], grad_rows[None], grad_phi_t, grad_up[None], grad_down[None])


def solution(mesh):
    fine = Mesh(mesh.devices.reshape(4, 4, 4, 2), ("x", "y", "z", "core"))
    rows = P(GROUP, "x", None)
    blocks = P(("x",) + GROUP, None, None)
    return jax.shard_map(
        per_device,
        mesh=fine,
        in_specs=(rows, P(GROUP, "x"), P(None, GROUP), blocks, blocks, rows),
        out_specs=(rows, rows, P(("x",) + GROUP, None), blocks, blocks),
        check_vma=False,
    )
```
